1024 devices in a mesh: row: 16 (over z_lo), col: 64 (over z_hi, x, y, core).
Axes of the slice: x: 4, y: 4, z: 32 (z_hi: 2, z_lo: 16; z = z_hi * 16 + z_lo), core: 2. Of those that a mesh axis runs over, the one named last changes fastest.
Arguments:
- photo_features: bfloat16 [12288, 1152], P(('row', 'col')), may hold values from -6 to 6
- sentence_features: bfloat16 [12288, 1152], P(('row', 'col')), may hold values from -6 to 6
- described_photo_number: int32 [12288], P(('row', 'col')), may hold values from 0 to 12287, each once
- logit_multiplier: float32 [], replicated, may hold values from 3 to 8
- logit_offset: float32 [], replicated, may hold values from -4 to -1
Outputs:
- img_grad: float32 [12288, 1152], P(('row', 'col'))
- txt_grad: float32 [12288, 1152], P(('row', 'col'))
The draws below stay inside these ranges and needn't reach their ends.
Inputs may be any that keep to these rules, and one draw needn't show every extreme that they name: `described_photo_number`: every image index appears exactly once among the text ids.
All inputs are finite; a program needn't handle non-finite values.
Results may differ from the reference program's by a relative error of at most 0.004.
Values may be sent and summed in bfloat16 or wider, within the bound.
No kernel may reach another device: no remote copies, remote signals or barrier semaphores. Data moves between devices by JAX's collectives and lax.ppermute only.
A program may use at most 32 MiB of HBM per device.

```python
import jax
import jax.numpy as jnp
from jax import lax

D = 1152
PAIRS = 12288
N_ROW = 16


def level_of(key, extent, split, low, top_value):
    gain = 1.0
    for dim, shards_of in split:
        steps = jax.random.uniform(jax.random.fold_in(jax.random.fold_in(key, 6), dim), (shards_of,), jnp.float32, low / len(split), top_value / len(split))
        gain = gain * jnp.repeat(jnp.exp(steps), extent[dim] // shards_of).reshape((-1,) + (1,) * (len(extent) - 1 - dim))
    return gain


def centred(key, extent, deviation, most, split=(), held_as=jnp.bfloat16):
    drawn = deviation * jax.random.normal(key, extent, jnp.float32)
    if split:
        drawn = drawn * level_of(key, extent, split, -0.22, 0.18)
    return jnp.clip(drawn, -most, most).astype(held_as)


def setup_inputs(seed: int = 0) -> dict:
    key_list = jax.random.split(jax.random.key(seed), 6)
    photo_features = centred(key_list[0], (PAIRS, D), 1.0, 6.0, ((0, 1024),))
    sentence_features = centred(key_list[1], (PAIRS, D), 1.0, 6.0, ((0, 1024),))
    described_photo_number = jax.random.permutation(key_list[2], PAIRS).astype(jnp.int32)
    logit_multiplier = jnp.clip(jax.random.uniform(key_list[3], (), jnp.float32, 3.0, 8.0), 3.0, 8.0)
    logit_offset = jnp.clip(jax.random.uniform(key_list[4], (), jnp.float32, -4.0, -1.0), -4.0, -1.0)
    return dict(photo_features=photo_features, sentence_features=sentence_features, described_photo_number=described_photo_number, logit_multiplier=logit_multiplier, logit_offset=logit_offset)


def unit_rows(raw):
    values = raw.astype(jnp.float32)
    scale = lax.rsqrt(lax.optimization_barrier(jnp.sum(values * values, axis=1, keepdims=True)) + 1e-06)
    return (values * scale, scale)

def back_through(unit, scale, upstream):
    inner = lax.optimization_barrier(jnp.sum(unit * upstream, axis=1, keepdims=True))
    return scale * (upstream - unit * inner)

def reference(photo_features, sentence_features, described_photo_number, logit_multiplier, logit_offset):
    img_unit, img_scale = unit_rows(photo_features)
    txt_unit, txt_scale = unit_rows(sentence_features)
    img_send = img_unit.astype(jnp.bfloat16)
    sentence_sent_onward = txt_unit.astype(jnp.bfloat16)
    block_rows = PAIRS // N_ROW

    def one_block(txt_acc, index):
        start = (index * block_rows).astype(jnp.int32)
        photo_entries = lax.dynamic_slice_in_dim(img_send, start, block_rows, 0)
        similarity_logits = logit_multiplier * jnp.dot(photo_entries, sentence_sent_onward.T, preferred_element_type=jnp.float32) + logit_offset
        ids = start + lax.iota(jnp.int32, block_rows)
        match_polarity = jnp.where(ids[:, None] == described_photo_number[None, :], 1.0, -1.0).astype(similarity_logits.dtype)
        coefficient_table = (logit_multiplier * -match_polarity * jax.nn.sigmoid(-match_polarity * similarity_logits)).astype(jnp.bfloat16)
        img_up = jnp.dot(coefficient_table, sentence_sent_onward, preferred_element_type=jnp.float32)
        txt_acc = txt_acc + jnp.dot(coefficient_table.T, photo_entries, preferred_element_type=jnp.float32)
        return (txt_acc, img_up)
    start_acc = jnp.zeros((PAIRS, D), jnp.float32)
    txt_upstream, img_parts = lax.scan(one_block, start_acc, jnp.arange(N_ROW, dtype=jnp.int32))
    img_upstream = img_parts.reshape(PAIRS, D)
    return (back_through(img_unit, img_scale, img_upstream), back_through(txt_unit, txt_scale, txt_upstream))
```

```python
import jax
import jax.numpy as jnp
from jax import lax
from jax.sharding import PartitionSpec as P

NZ, NX, NY, NC = 32, 4, 4, 2
OWN = 12
SLOT = 16
BOTH = ("row", "col")


def device_at(z, x, y, c):
    return (z % 16) * 64 + (z // 16) * 32 + x * 8 + y * 2 + c


def send(value, dz=0, dx=0, dy=0, dc=0):
    pairs = [
        (
            device_at(z, x, y, c),
            device_at((z + dz) % NZ, (x + dx) % NX, (y + dy) % NY, (c + dc) % NC),
        )
        for z in range(NZ)
        for x in range(NX)
        for y in range(NY)
        for c in range(NC)
    ]
    return lax.ppermute(value, BOTH, pairs)


IMG_Z = (0, 16, -2, 14)
TXT_Z = (0, 8, 4, 12, 1, 9, 5, 13)
RING = (0, 1, -1, 2)


def unit_rows(raw):
    values = raw.astype(jnp.float32)
    scale = lax.rsqrt(jnp.sum(values * values, axis=1, keepdims=True) + 1e-06)
    return (values * scale, scale)


def back_through(unit, scale, upstream):
    inner = jnp.sum(unit * upstream, axis=1, keepdims=True)
    return scale * (upstream - unit * inner)


def cat(*parts):
    return jnp.concatenate(parts, axis=0)


def gather_images(block):
    with jax.named_scope("img_z16"):
        block = cat(block, send(block, dz=16))
    with jax.named_scope("img_z2"):
        block = cat(block, send(block, dz=2))
    with jax.named_scope("img_x"):
        block = cat(block, *(send(block, dx=-k) for k in RING[1:]))
    with jax.named_scope("img_core"):
        return cat(block, send(block, dc=1))


def gather_texts(block):
    with jax.named_scope("txt_z8"):
        block = cat(block, send(block, dz=-8))
    with jax.named_scope("txt_z4"):
        block = cat(block, send(block, dz=-4))
    with jax.named_scope("txt_z1"):
        block = cat(block, send(block, dz=-1))
    with jax.named_scope("txt_y"):
        return cat(block, *(send(block, dy=-k) for k in RING[1:]))


def halve(total, **shift):
    rows = total.shape[0] // 2
    return total[:rows] + send(total[rows:].astype(jnp.bfloat16), **shift).astype(jnp.float32)


def quarter(total, axis):
    rows = total.shape[0] // 4
    acc = total[:rows]
    for g in (1, 2, 3):
        part = total[g * rows : (g + 1) * rows].astype(jnp.bfloat16)
        acc = acc + send(part, **{axis: RING[g]}).astype(jnp.float32)
    return acc


def reduce_images(total):
    with jax.named_scope("img_core_sum"):
        total = halve(total, dc=1)
    with jax.named_scope("img_x_sum"):
        total = quarter(total, "dx")
    with jax.named_scope("img_z2_sum"):
        total = halve(total, dz=-2)
    with jax.named_scope("img_z16_sum"):
        return halve(total, dz=16)


def reduce_texts(total):
    with jax.named_scope("txt_y_sum"):
        total = quarter(total, "dy")
    with jax.named_scope("txt_z1_sum"):
        total = halve(total, dz=1)
    with jax.named_scope("txt_z4_sum"):
        total = halve(total, dz=4)
    with jax.named_scope("txt_z8_sum"):
        return halve(total, dz=8)


def image_ids(z, x, y, c):
    row = lax.iota(jnp.int32, 32 * SLOT)
    r = row % SLOT
    slot = row // SLOT
    zslot, xslot, cslot = slot % 4, (slot // 4) % 4, slot // 16
    zoff = jnp.where(zslot % 2 == 1, 16, 0) + jnp.where(zslot >= 2, NZ - 2, 0)
    xoff = jnp.where(xslot == 1, 1, jnp.where(xslot == 2, NX - 1, jnp.where(xslot == 3, 2, 0)))
    owner = device_at((z + zoff) % NZ, (x + xoff) % NX, y, (c + cslot) % NC)
    return jnp.where(r < OWN, owner * OWN + r, -1)


def shards(
    photo_features, sentence_features, described_photo_number, logit_multiplier, logit_offset
):
    img_unit, img_scale = unit_rows(photo_features)
    txt_unit, txt_scale = unit_rows(sentence_features)
    pad = SLOT - OWN
    img_block = jnp.pad(img_unit.astype(jnp.bfloat16), ((0, pad), (0, 0)))
    width = txt_unit.shape[1]
    ids = jnp.stack([described_photo_number // 128, described_photo_number % 128])
    ids = jnp.pad(ids.astype(jnp.bfloat16), ((0, pad - 2), (0, width - OWN)))
    txt_block = cat(txt_unit.astype(jnp.bfloat16), ids)

    imgs = gather_images(img_block)
    txts = gather_texts(txt_block)

    low = lax.axis_index("row")
    rest = lax.axis_index("col")
    z, x, y, c = (rest // 32) * 16 + low, (rest // 8) % 4, (rest // 2) % 4, rest % 2
    coded = txts.reshape(32, SLOT, width)[:, OWN : OWN + 2, :OWN].astype(jnp.int32)
    numbers = jnp.pad(coded[:, 0] * 128 + coded[:, 1], ((0, 0), (0, pad)), constant_values=-2)
    numbers = numbers.reshape(32 * SLOT)
    used = lax.iota(jnp.int32, 32 * SLOT) % SLOT < OWN
    txts = jnp.where(used[:, None], txts, jnp.zeros_like(txts))

    logits = (
        logit_multiplier
        * jnp.einsum("id,jd->ij", imgs, txts, preferred_element_type=jnp.float32)
        + logit_offset
    )
    ids = image_ids(z, x, y, c)
    sign = jnp.where(ids[:, None] == numbers[None, :], 1.0, -1.0).astype(jnp.float32)
    weights = (logit_multiplier * -sign * jax.nn.sigmoid(-sign * logits)).astype(jnp.bfloat16)
    txt_part = jnp.einsum("ij,id->jd", weights, imgs, preferred_element_type=jnp.float32)
    img_part = jnp.dot(weights, txts, preferred_element_type=jnp.float32)

    img_upstream = reduce_images(img_part)[:OWN]
    txt_upstream = reduce_texts(txt_part)[:OWN]
    return (
        back_through(img_unit, img_scale, img_upstream),
        back_through(txt_unit, txt_scale, txt_upstream),
    )


def solution(mesh):
    placed = (P(("row", "col"), None), P(("row", "col"), None), P(("row", "col")), P(), P())
    return jax.shard_map(
        shards,
        mesh=mesh,
        in_specs=placed,
        out_specs=(P(("row", "col"), None), P(("row", "col"), None)),
        check_vma=False,
    )
```

```python
import jax
import jax.numpy as jnp
from jax import lax
from jax.sharding import PartitionSpec as P

NZ, NX, NY = 32, 4, 4
OWN = 12
CHIP = 2 * OWN
LANES = 128
BOTH = ("row", "col")
RING = (0, 1, NX - 1, 2)


def device_at(z, x, y, c):
    return (z & 15) * 64 + (z >> 4) * 32 + x * 8 + y * 2 + c


def permute(value, images=None, texts=None):
    pairs = []
    for z in range(NZ):
        for x in range(NX):
            for y in range(NY):
                for c, to in enumerate((images, texts)):
                    if to is not None:
                        pairs.append((device_at(z, x, y, c), device_at(*to(z, x, y), c)))
    return lax.ppermute(value, BOTH, pairs)


def z_far(value):
    return permute(
        value,
        lambda z, x, y: (z ^ 8, x, y),
        lambda z, x, y: ((((z + 8) % NZ) ^ 8) - 8 & (NZ - 1), x, y),
    )


def z_mid(value):
    return permute(value, lambda z, x, y: (z ^ 2, x, y), lambda z, x, y: (z ^ 4, x, y))


def z_near(value):
    return permute(value, None, lambda z, x, y: (z ^ 1, x, y))


def along_ring(value, shift):
    return permute(
        value,
        lambda z, x, y: (z, (x + shift) % NX, y),
        lambda z, x, y: (z, x, (y + shift) % NY),
    )


def swap_cores(value):
    n = NZ * NX * NY * 2
    return lax.ppermute(value, BOTH, [(d, d ^ 1) for d in range(n)])


def unit_rows(raw):
    values = raw.astype(jnp.float32)
    scale = lax.rsqrt(jnp.sum(values * values, axis=1, keepdims=True) + 1e-06)
    return (values * scale, scale)


def back_through(unit, scale, upstream):
    inner = jnp.sum(unit * upstream, axis=1, keepdims=True)
    return scale * (upstream - unit * inner)


def cat(*parts):
    return jnp.concatenate(parts, axis=0)


def image_ids(z, x, y):
    row = lax.iota(jnp.int32, 16 * CHIP)
    group, zslot, r = row // (4 * CHIP), row // CHIP % 4, row % CHIP
    owner_z = z ^ jnp.where(zslot % 2 == 1, 8, 0) ^ jnp.where(zslot >= 2, 2, 0)
    step = jnp.where(group == 1, RING[1], jnp.where(group == 2, RING[2], jnp.where(group == 3, RING[3], 0)))
    owner = device_at(owner_z, (x + step) & (NX - 1), y, r // OWN)
    return owner * OWN + r % OWN


def shards(
    photo_features, sentence_features, described_photo_number, logit_multiplier, logit_offset
):
    low = lax.axis_index("row")
    rest = lax.axis_index("col")
    z, x, y = (rest >> 5) * 16 + low, (rest >> 3) & 3, (rest >> 1) & 3
    holds_images = (rest & 1) == 0

    img_unit, img_scale = unit_rows(photo_features)
    txt_unit, txt_scale = unit_rows(sentence_features)
    width = img_unit.shape[1]
    ids = jnp.stack([described_photo_number // 128, described_photo_number % 128], axis=1)
    ids = jnp.pad(ids.astype(jnp.bfloat16), ((0, 0), (0, LANES - 2)))
    img_block = jnp.pad(img_unit.astype(jnp.bfloat16), ((0, 0), (0, LANES)))
    txt_block = jnp.concatenate([txt_unit.astype(jnp.bfloat16), ids], axis=1)

    with jax.named_scope("pair_swap"):
        given = swap_cores(jnp.where(holds_images, txt_block, img_block))
        block = cat(jnp.where(holds_images, img_block, txt_block), given)
    with jax.named_scope("gather_z_far"):
        block = cat(block, z_far(block))
    with jax.named_scope("gather_z_mid"):
        block = cat(block, z_mid(block))
    with jax.named_scope("gather_z_near"):
        block = cat(block, z_near(block))
    with jax.named_scope("gather_ring"):
        groups = [block] + [along_ring(block, -k) for k in RING[1:]]
    half = 4 * CHIP
    with jax.named_scope("tile_swap"):
        first = cat(*(g[:half] for g in groups))
        other = swap_cores(first)
        second = cat(*(g[half:] for g in groups))

    imgs = jnp.where(holds_images, first, other)[:, :width]
    coded = jnp.where(holds_images, other, second)
    txts = coded[:, :width]
    numbers = coded[:, width].astype(jnp.int32) * 128 + coded[:, width + 1].astype(jnp.int32)

    logits = (
        logit_multiplier
        * jnp.einsum("jd,id->ji", txts, imgs, preferred_element_type=jnp.float32)
        + logit_offset
    )
    sign = jnp.where(numbers[:, None] == image_ids(z, x, y)[None, :], 1.0, -1.0).astype(jnp.float32)
    weights = (logit_multiplier * -sign * jax.nn.sigmoid(-sign * logits)).astype(jnp.bfloat16)
    txt_part = jnp.dot(weights, imgs, preferred_element_type=jnp.float32)
    img_part = jnp.einsum("ji,jd->id", weights, txts, preferred_element_type=jnp.float32)

    with jax.named_scope("tile_sum"):
        away = jnp.where(holds_images, txt_part, img_part).astype(jnp.bfloat16)
        home = jnp.where(holds_images, img_part, jnp.zeros_like(img_part))
        first = home + swap_cores(away).astype(jnp.float32)
    with jax.named_scope("ring_sum"):
        total = cat(first[:half], txt_part[:half])
        for g in (1, 2, 3):
            rows = slice(g * half, (g + 1) * half)
            part = cat(first[rows], txt_part[rows]).astype(jnp.bfloat16)
            total = total + along_ring(part, RING[g]).astype(jnp.float32)
    for name, swap in (("z_near_sum", z_near), ("z_mid_sum", z_mid), ("z_far_sum", z_far)):
        with jax.named_scope(name):
            rows = total.shape[0] // 2
            total = total[:rows] + swap(total[rows:].astype(jnp.bfloat16)).astype(jnp.float32)
    with jax.named_scope("pair_return"):
        kept, given = total[:OWN], swap_cores(total[OWN:])
    return (
        back_through(img_unit, img_scale, jnp.where(holds_images, kept, given)),
        back_through(txt_unit, txt_scale, jnp.where(holds_images, given, kept)),
    )


def solution(mesh):
    placed = (P(("row", "col"), None), P(("row", "col"), None), P(("row", "col")), P(), P())
    return jax.shard_map(
        shards,
        mesh=mesh,
        in_specs=placed,
        out_specs=(P(("row", "col"), None), P(("row", "col"), None)),
        check_vma=False,
    )
```

```python
import jax
import jax.numpy as jnp
from jax import lax
from jax.sharding import PartitionSpec as P

NZ, NX, NY = 32, 4, 4
OWN = 12
CHIP = 2 * OWN
LANES = 128
BOTH = ("row", "col")
RING = (0, 1, NX - 1, 2)


def device_at(z, x, y, c):
    return (z & 15) * 64 + (z >> 4) * 32 + x * 8 + y * 2 + c


def permute(value, images=None, texts=None):
    pairs = []
    for z in range(NZ):
        for x in range(NX):
            for y in range(NY):
                for c, to in enumerate((images, texts)):
                    if to is not None:
                        pairs.append((device_at(z, x, y, c), device_at(*to(z, x, y), c)))
    return lax.ppermute(value, BOTH, pairs)


def z_far(value):
    return permute(
        value,
        lambda z, x, y: (z ^ 8, x, y),
        lambda z, x, y: ((((z + 8) % NZ) ^ 8) - 8 & (NZ - 1), x, y),
    )


def z_mid(value):
    return permute(value, lambda z, x, y: (z ^ 2, x, y), lambda z, x, y: (z ^ 4, x, y))


def along_ring(value, shift):
    return permute(
        value,
        lambda z, x, y: (z, (x + shift) % NX, y),
        lambda z, x, y: (z, x, (y + shift) % NY),
    )


def swap_cores(value):
    n = NZ * NX * NY * 2
    return lax.ppermute(value, BOTH, [(d, d ^ 1) for d in range(n)])


def cross(value, back=False):
    pairs = []
    for z in range(NZ):
        for x in range(NX):
            for y in range(NY):
                pairs.append((device_at(z, x, y, 1), device_at(z, x, y, 0)))
                pairs.append((device_at(z, x, y, 0), device_at(z ^ 1, x, y, 1)))
    return lax.ppermute(value, BOTH, [(b, a) for a, b in pairs] if back else pairs)


def unit_rows(raw):
    values = raw.astype(jnp.float32)
    scale = lax.rsqrt(jnp.sum(values * values, axis=1, keepdims=True) + 1e-06)
    return (values * scale, scale)


def back_through(unit, scale, upstream):
    inner = jnp.sum(unit * upstream, axis=1, keepdims=True)
    return scale * (upstream - unit * inner)


def cat(*parts):
    return jnp.concatenate(parts, axis=0)


def image_ids(z, x, y):
    row = lax.iota(jnp.int32, 16 * CHIP)
    group, zslot, r = row // (4 * CHIP), row // CHIP % 4, row % CHIP
    owner_z = z ^ jnp.where(zslot % 2 == 1, 8, 0) ^ jnp.where(zslot >= 2, 2, 0)
    step = jnp.where(group == 1, RING[1], jnp.where(group == 2, RING[2], jnp.where(group == 3, RING[3], 0)))
    owner = device_at(owner_z, (x + step) & (NX - 1), y, r // OWN)
    return owner * OWN + r % OWN


def shards(
    photo_features, sentence_features, described_photo_number, logit_multiplier, logit_offset
):
    low = lax.axis_index("row")
    rest = lax.axis_index("col")
    z, x, y = (rest >> 5) * 16 + low, (rest >> 3) & 3, (rest >> 1) & 3
    holds_images = (rest & 1) == 0

    img_unit, img_scale = unit_rows(photo_features)
    txt_unit, txt_scale = unit_rows(sentence_features)
    width = img_unit.shape[1]
    ids = jnp.stack([described_photo_number // 128, described_photo_number % 128], axis=1)
    ids = jnp.pad(ids.astype(jnp.bfloat16), ((0, 0), (0, LANES - 2)))
    img_block = jnp.pad(img_unit.astype(jnp.bfloat16), ((0, 0), (0, LANES)))
    txt_block = jnp.concatenate([txt_unit.astype(jnp.bfloat16), ids], axis=1)

    with jax.named_scope("pair_swap"):
        given = swap_cores(jnp.where(holds_images, txt_block, img_block))
        block = cat(jnp.where(holds_images, img_block, txt_block), given)
    with jax.named_scope("gather_z_far"):
        block = cat(block, z_far(block))
    with jax.named_scope("gather_z_mid"):
        block = cat(block, z_mid(block))
    with jax.named_scope("gather_ring"):
        groups = [block] + [along_ring(block, -k) for k in RING[1:]]
    with jax.named_scope("tile_cross"):
        crossed = cat(*(cross(g) for g in groups))
        held = cat(*groups)

    imgs = jnp.where(holds_images, held, crossed)[:, :width]
    coded = jnp.where(holds_images, crossed, held)
    txts = coded[:, :width]
    numbers = coded[:, width].astype(jnp.int32) * 128 + coded[:, width + 1].astype(jnp.int32)
    img_z = jnp.where(holds_images, z, z ^ 1)

    logits = (
        logit_multiplier
        * jnp.einsum("jd,id->ji", txts, imgs, preferred_element_type=jnp.float32)
        + logit_offset
    )
    sign = jnp.where(numbers[:, None] == image_ids(img_z, x, y)[None, :], 1.0, -1.0).astype(jnp.float32)
    weights = (logit_multiplier * -sign * jax.nn.sigmoid(-sign * logits)).astype(jnp.bfloat16)
    txt_part = jnp.dot(weights, imgs, preferred_element_type=jnp.float32)
    img_part = jnp.einsum("ji,jd->id", weights, txts, preferred_element_type=jnp.float32)

    half = 4 * CHIP
    away = jnp.where(holds_images, txt_part, img_part).astype(jnp.bfloat16)
    home = jnp.where(holds_images, img_part, txt_part)
    sums = []
    for g in range(4):
        with jax.named_scope("tile_sum"):
            rows = slice(g * half, (g + 1) * half)
            sums.append(home[rows] + cross(away[rows], back=True).astype(jnp.float32))
    with jax.named_scope("ring_sum"):
        total = sums[0]
        for g in (1, 2, 3):
            total = total + along_ring(sums[g].astype(jnp.bfloat16), RING[g]).astype(jnp.float32)
    for name, swap in (("z_mid_sum", z_mid), ("z_far_sum", z_far)):
        with jax.named_scope(name):
            rows = total.shape[0] // 2
            total = total[:rows] + swap(total[rows:].astype(jnp.bfloat16)).astype(jnp.float32)
    with jax.named_scope("pair_return"):
        kept, given = total[:OWN], swap_cores(total[OWN:])
    return (
        back_through(img_unit, img_scale, jnp.where(holds_images, kept, given)),
        back_through(txt_unit, txt_scale, jnp.where(holds_images, given, kept)),
    )


def solution(mesh):
    placed = (P(("row", "col"), None), P(("row", "col"), None), P(("row", "col")), P(), P())
    return jax.shard_map(
        shards,
        mesh=mesh,
        in_specs=placed,
        out_specs=(P(("row", "col"), None), P(("row", "col"), None)),
        check_vma=False,
    )
```

```python
import jax
import jax.numpy as jnp
from jax import lax
from jax.sharding import PartitionSpec as P

NZ, NX, NY = 32, 4, 4
OWN = 12
CHIP = 2 * OWN
LANES = 128
BOTH = ("row", "col")
RING = (0, 1, NX - 1, 2)


def device_at(z, x, y, c):
    return (z & 15) * 64 + (z >> 4) * 32 + x * 8 + y * 2 + c


def permute(value, images=None, texts=None):
    pairs = []
    for z in range(NZ):
        for x in range(NX):
            for y in range(NY):
                for c, to in enumerate((images, texts)):
                    if to is not None:
                        pairs.append((device_at(z, x, y, c), device_at(*to(z, x, y), c)))
    return lax.ppermute(value, BOTH, pairs)


def z_far(value):
    return permute(
        value,
        lambda z, x, y: (z ^ 8, x, y),
        lambda z, x, y: ((((z + 8) % NZ) ^ 8) - 8 & (NZ - 1), x, y),
    )


def z_mid(value):
    return permute(value, lambda z, x, y: (z ^ 2, x, y), lambda z, x, y: (z ^ 4, x, y))


def along_ring(value, shift):
    return permute(
        value,
        lambda z, x, y: (z, (x + shift) % NX, y),
        lambda z, x, y: (z, x, (y + shift) % NY),
    )


def swap_cores(value):
    n = NZ * NX * NY * 2
    return lax.ppermute(value, BOTH, [(d, d ^ 1) for d in range(n)])


def cross(value, back=False):
    pairs = []
    for z in range(NZ):
        for x in range(NX):
            for y in range(NY):
                pairs.append((device_at(z, x, y, 1), device_at(z, x, y, 0)))
                pairs.append((device_at(z, x, y, 0), device_at(z ^ 1, x, y, 1)))
    return lax.ppermute(value, BOTH, [(b, a) for a, b in pairs] if back else pairs)


def unit_rows(raw):
    values = raw.astype(jnp.float32)
    scale = lax.rsqrt(jnp.sum(values * values, axis=1, keepdims=True) + 1e-06)
    return (values * scale, scale)


def back_through(unit, scale, upstream):
    inner = jnp.sum(unit * upstream, axis=1, keepdims=True)
    return scale * (upstream - unit * inner)


def cat(*parts):
    return jnp.concatenate(parts, axis=0)


def image_ids(z, x, y):
    row = lax.iota(jnp.int32, 16 * CHIP)
    group, zslot, r = row // (4 * CHIP), row // CHIP % 4, row % CHIP
    owner_z = z ^ jnp.where(zslot % 2 == 1, 8, 0) ^ jnp.where(zslot >= 2, 2, 0)
    step = jnp.where(group == 1, RING[1], jnp.where(group == 2, RING[2], jnp.where(group == 3, RING[3], 0)))
    owner = device_at(owner_z, (x + step) & (NX - 1), y, r // OWN)
    return owner * OWN + r % OWN


def shards(
    photo_features, sentence_features, described_photo_number, logit_multiplier, logit_offset
):
    low = lax.axis_index("row")
    rest = lax.axis_index("col")
    z, x, y = (rest >> 5) * 16 + low, (rest >> 3) & 3, (rest >> 1) & 3
    holds_images = (rest & 1) == 0

    img_unit, img_scale = unit_rows(photo_features)
    txt_unit, txt_scale = unit_rows(sentence_features)
    width = img_unit.shape[1]
    ids = jnp.stack([described_photo_number // 128, described_photo_number % 128], axis=1)
    ids = jnp.pad(ids.astype(jnp.bfloat16), ((0, 0), (0, LANES - 2)))
    img_block = jnp.pad(img_unit.astype(jnp.bfloat16), ((0, 0), (0, LANES)))
    txt_block = jnp.concatenate([txt_unit.astype(jnp.bfloat16), ids], axis=1)

    with jax.named_scope("pair_swap"):
        given = swap_cores(jnp.where(holds_images, txt_block, img_block))
        block = cat(jnp.where(holds_images, img_block, txt_block), given)
    with jax.named_scope("gather_z_far"):
        block = cat(block, z_far(block))
    with jax.named_scope("gather_z_mid"):
        block = cat(block, z_mid(block))
    with jax.named_scope("gather_ring"):
        groups = [block] + [along_ring(block, -k) for k in RING[1:]]
    with jax.named_scope("tile_cross"):
        parts = [cross(groups[0])]
        for g in groups[1:]:
            g, parts[0] = lax.optimization_barrier((g, parts[0]))
            parts.append(cross(g))
        crossed = cat(*parts)
        held = cat(*groups)

    imgs = jnp.where(holds_images, held, crossed)[:, :width]
    coded = jnp.where(holds_images, crossed, held)
    txts = coded[:, :width]
    numbers = coded[:, width].astype(jnp.int32) * 128 + coded[:, width + 1].astype(jnp.int32)
    img_z = jnp.where(holds_images, z, z ^ 1)

    logits = (
        logit_multiplier
        * jnp.einsum("jd,id->ji", txts, imgs, preferred_element_type=jnp.float32)
        + logit_offset
    )
    sign = jnp.where(numbers[:, None] == image_ids(img_z, x, y)[None, :], 1.0, -1.0).astype(jnp.float32)
    weights = (logit_multiplier * -sign * jax.nn.sigmoid(-sign * logits)).astype(jnp.bfloat16)
    txt_part = jnp.dot(weights, imgs, preferred_element_type=jnp.float32)
    img_part = jnp.einsum("ji,jd->id", weights, txts, preferred_element_type=jnp.float32)

    half = 4 * CHIP
    away = jnp.where(holds_images, txt_part, img_part).astype(jnp.bfloat16)
    home = jnp.where(holds_images, img_part, txt_part)
    with jax.named_scope("tile_sum"):
        crossed = [cross(away[g * half : (g + 1) * half], back=True) for g in range(4)]
    with jax.named_scope("ring_sum"):
        arrived = []
        for g in (1, 2, 3):
            part = (home[g * half : (g + 1) * half] + crossed[g].astype(jnp.float32)).astype(jnp.bfloat16)
            part, home, early = lax.optimization_barrier((part, home, arrived[:1] if g == 3 else []))
            arrived[: len(early)] = early
            arrived.append(along_ring(part, RING[g]))
        total = home[:half] + crossed[0].astype(jnp.float32)
        for part in arrived:
            total = total + part.astype(jnp.float32)
    for name, swap in (("z_mid_sum", z_mid), ("z_far_sum", z_far)):
        with jax.named_scope(name):
            rows = total.shape[0] // 2
            total = total[:rows] + swap(total[rows:].astype(jnp.bfloat16)).astype(jnp.float32)
    with jax.named_scope("pair_return"):
        kept, given = total[:OWN], swap_cores(total[OWN:])
    return (
        back_through(img_unit, img_scale, jnp.where(holds_images, kept, given)),
        back_through(txt_unit, txt_scale, jnp.where(holds_images, given, kept)),
    )


def solution(mesh):
    placed = (P(("row", "col"), None), P(("row", "col"), None), P(("row", "col")), P(), P())
    return jax.shard_map(
        shards,
        mesh=mesh,
        in_specs=placed,
        out_specs=(P(("row", "col"), None), P(("row", "col"), None)),
        check_vma=False,
    )
```

```python
import jax
import jax.numpy as jnp
from jax import lax
from jax.experimental import pallas as pl
from jax.experimental.pallas import tpu as pltpu
from jax.sharding import PartitionSpec as P

NZ, NX, NY = 32, 4, 4
OWN = 12
CHIP = 2 * OWN
LANES = 128
BOTH = ("row", "col")


def device_at(z, x, y, c):
    return (z & 15) * 64 + (z >> 4) * 32 + x * 8 + y * 2 + c


def permute(value, images=None, texts=None):
    pairs = []
    for z in range(NZ):
        for x in range(NX):
            for y in range(NY):
                for c, to in enumerate((images, texts)):
                    if to is not None:
                        pairs.append((device_at(z, x, y, c), device_at(*to(z, x, y), c)))
    return lax.ppermute(value, BOTH, pairs)


def z_far(value):
    return permute(
        value,
        lambda z, x, y: (z ^ 8, x, y),
        lambda z, x, y: ((((z + 8) % NZ) ^ 8) - 8 & (NZ - 1), x, y),
    )


def z_mid(value):
    return permute(value, lambda z, x, y: (z ^ 2, x, y), lambda z, x, y: (z ^ 4, x, y))


def eights():
    groups, seen = [], set()
    for z in range(NZ):
        for k in range(4):
            for c in range(2):
                if (z, k, c) in seen:
                    continue
                pair = (z, z ^ 1) if c else (z, (z + 1 if z % 2 else z - 1) % NZ)
                seen.update((w, k, c) for w in pair)
                groups.append([device_at(w, *((k, n) if c else (n, k)), c) for w in pair for n in range(4)])
    return groups


EIGHTS = eights()


def around(value):
    return lax.all_to_all(value, BOTH, 0, 0, axis_index_groups=EIGHTS, tiled=True)


def swap_cores(value):
    n = NZ * NX * NY * 2
    return lax.ppermute(value, BOTH, [(d, d ^ 1) for d in range(n)])


def pack_kernel(photo, sentence, ids, own, given, img_scale, txt_scale):
    width = photo.shape[1]
    holds_images = lax.axis_index("col") % 2 == 0

    def unit(raw, scale):
        values = raw[...].astype(jnp.float32)
        scale[...] = lax.rsqrt(jnp.sum(values * values, axis=1, keepdims=True) + 1e-06)
        return values * scale[...]

    img, txt = unit(photo, img_scale), unit(sentence, txt_scale)
    square = (OWN, OWN)
    diagonal = lax.broadcasted_iota(jnp.int32, square, 0) == lax.broadcasted_iota(jnp.int32, square, 1)
    spread = jnp.broadcast_to(ids[...].astype(jnp.float32), square)
    number = jnp.sum(jnp.where(diagonal, spread, 0.0), axis=1, keepdims=True)
    high = jnp.floor(number * (1 / 128))
    lane = lax.broadcasted_iota(jnp.int32, (OWN, LANES), 1)
    tail = jnp.where(lane == 0, high, jnp.where(lane == 1, number - high * 128, 0.0))
    none = jnp.zeros_like(tail)
    own[:, :width] = jnp.where(holds_images, img, txt).astype(jnp.bfloat16)
    own[:, width:] = jnp.where(holds_images, none, tail).astype(jnp.bfloat16)
    given[:, :width] = jnp.where(holds_images, txt, img).astype(jnp.bfloat16)
    given[:, width:] = jnp.where(holds_images, tail, none).astype(jnp.bfloat16)


def pack_rows(photo_features, sentence_features, ids):
    rows, width = photo_features.shape
    block = jax.ShapeDtypeStruct((rows, width + LANES), jnp.bfloat16)
    scale = jax.ShapeDtypeStruct((rows, 1), jnp.float32)
    return pl.pallas_call(
        pack_kernel,
        out_shape=(block, block, scale, scale),
        compiler_params=pltpu.CompilerParams(vmem_limit_bytes=2 << 20),
        name="pack_rows",
    )(photo_features, sentence_features, ids.reshape(1, rows))


def back_through(raw, scale, upstream):
    unit = raw.astype(jnp.float32) * scale
    inner = jnp.sum(unit * upstream, axis=1, keepdims=True)
    return scale * (upstream - unit * inner)


def cat(*parts):
    return jnp.concatenate(parts, axis=0)


def image_ids(z, y):
    row = lax.iota(jnp.int32, 16 * CHIP)
    group, zslot, r = row // (4 * CHIP), row // CHIP % 4, row % CHIP
    owner_z = z ^ jnp.where(zslot % 2 == 1, 8, 0) ^ jnp.where(zslot >= 2, 2, 0)
    owner = device_at(owner_z, group, y, r // OWN)
    return owner * OWN + r % OWN


def text_ids(tail):
    place = lax.broadcasted_iota(jnp.int32, tail.shape, 1)
    weight = jnp.where(place == 0, 128.0, jnp.where(place == 1, 1.0, 0.0))
    return jnp.sum(tail.astype(jnp.float32) * weight, axis=1).astype(jnp.int32)


def shards(
    photo_features, sentence_features, described_photo_number, logit_multiplier, logit_offset
):
    low = lax.axis_index("row")
    rest = lax.axis_index("col")
    z, y = (rest >> 5) * 16 + low, (rest >> 1) & 3
    holds_images = (rest & 1) == 0

    width = photo_features.shape[1]
    block_own, block_given, img_scale, txt_scale = pack_rows(
        photo_features, sentence_features, described_photo_number
    )

    with jax.named_scope("pair_swap"):
        block = cat(block_own, swap_cores(block_given))
    with jax.named_scope("gather_z_far"):
        block = cat(block, z_far(block))
    with jax.named_scope("gather_z_mid"):
        block = cat(block, z_mid(block))
    with jax.named_scope("gather_ring"):
        block = lax.optimization_barrier(block)
        held = around(jnp.tile(block, (8, 1)))
        first, second = held[: 16 * CHIP], held[16 * CHIP :]
    stands_first = (z == 0) | ((z % 2 == 1) & (z < NZ - 1))
    with jax.named_scope("tile_swap"):
        away_first = jnp.where(holds_images, stands_first, True)
        held = jnp.where(holds_images & stands_first, first, second)
        crossed = swap_cores(jnp.where(away_first, first, second))

    mine, other = held[:, :width], crossed[:, :width]
    img_ids = image_ids(z, y)
    mine_ids = jnp.where(holds_images, img_ids, text_ids(held[:, width:]))
    other_ids = jnp.where(holds_images, text_ids(crossed[:, width:]), img_ids)

    logits = (
        logit_multiplier
        * jnp.einsum("od,md->om", other, mine, preferred_element_type=jnp.float32)
        + logit_offset
    )
    sign = jnp.where(other_ids[:, None] == mine_ids[None, :], 1.0, -1.0).astype(jnp.float32)
    weights = (logit_multiplier * -sign * jax.nn.sigmoid(-sign * logits)).astype(jnp.bfloat16)
    away = jnp.dot(weights, mine, preferred_element_type=jnp.float32).astype(jnp.bfloat16)
    home = jnp.einsum("om,od->md", weights, other, preferred_element_type=jnp.float32)

    with jax.named_scope("tile_sum"):
        crossed = swap_cores(away).astype(jnp.float32)
        imgs, none = home + crossed, jnp.zeros_like(home)
        first = jnp.where(holds_images, jnp.where(stands_first, imgs, none), crossed)
        second = jnp.where(holds_images, jnp.where(stands_first, none, imgs), home)
    with jax.named_scope("ring_sum"):
        parts = around(cat(first.astype(jnp.bfloat16), second.astype(jnp.bfloat16)))
        total = jnp.sum(parts.reshape(8, 4 * CHIP, width).astype(jnp.float32), axis=0)
    for name, swap in (("z_mid_sum", z_mid), ("z_far_sum", z_far)):
        with jax.named_scope(name):
            rows = total.shape[0] // 2
            total = total[:rows] + swap(total[rows:].astype(jnp.bfloat16)).astype(jnp.float32)
    with jax.named_scope("pair_return"):
        kept, given = total[:OWN], swap_cores(total[OWN:])
    return (
        back_through(photo_features, img_scale, jnp.where(holds_images, kept, given)),
        back_through(sentence_features, txt_scale, jnp.where(holds_images, given, kept)),
    )


def solution(mesh):
    placed = (P(("row", "col"), None), P(("row", "col"), None), P(("row", "col")), P(), P())
    return jax.shard_map(
        shards,
        mesh=mesh,
        in_specs=placed,
        out_specs=(P(("row", "col"), None), P(("row", "col"), None)),
        check_vma=False,
    )
```

```python
import jax
import jax.numpy as jnp
from jax import lax
from jax.experimental import pallas as pl
from jax.experimental.pallas import tpu as pltpu
from jax.sharding import PartitionSpec as P

NZ, NX, NY = 32, 4, 4
OWN = 12
CHIP = 2 * OWN
LANES = 128
BOTH = ("row", "col")


def device_at(z, x, y, c):
    return (z & 15) * 64 + (z >> 4) * 32 + x * 8 + y * 2 + c


def permute(value, images=None, texts=None):
    pairs = []
    for z in range(NZ):
        for x in range(NX):
            for y in range(NY):
                for c, to in enumerate((images, texts)):
                    if to is not None:
                        pairs.append((device_at(z, x, y, c), device_at(*to(z, x, y), c)))
    return lax.ppermute(value, BOTH, pairs)


def z_far(value):
    return permute(
        value,
        lambda z, x, y: (z ^ 8, x, y),
        lambda z, x, y: ((((z + 8) % NZ) ^ 8) - 8 & (NZ - 1), x, y),
    )


def z_mid(value):
    return permute(value, lambda z, x, y: (z ^ 2, x, y), lambda z, x, y: (z ^ 4, x, y))


def eights():
    groups, seen = [], set()
    for z in range(NZ):
        for k in range(4):
            for c in range(2):
                if (z, k, c) in seen:
                    continue
                pair = (z, z ^ 1) if c else (z, (z + 1 if z % 2 else z - 1) % NZ)
                seen.update((w, k, c) for w in pair)
                groups.append([device_at(w, *((k, n) if c else (n, k)), c) for w in pair for n in range(4)])
    return groups


EIGHTS = eights()


def around(value):
    return lax.all_to_all(value, BOTH, 0, 0, axis_index_groups=EIGHTS, tiled=True)


def swap_cores(value):
    n = NZ * NX * NY * 2
    return lax.ppermute(value, BOTH, [(d, d ^ 1) for d in range(n)])


def pack_kernel(
    photo_in, sentence_in, ids_in, own, given, img_scale, txt_scale, photo, sentence, ids, arrived
):
    copies = [
        pltpu.make_async_copy(source, target, arrived.at[k])
        for k, (source, target) in enumerate(
            ((photo_in, photo), (sentence_in, sentence), (ids_in, ids))
        )
    ]
    for copy in copies:
        copy.start()
    for copy in copies:
        copy.wait()
    width = photo.shape[1]
    holds_images = lax.axis_index("col") % 2 == 0

    def unit(raw, scale):
        values = raw[...].astype(jnp.float32)
        scale[...] = lax.rsqrt(jnp.sum(values * values, axis=1, keepdims=True) + 1e-06)
        return values * scale[...]

    img, txt = unit(photo, img_scale), unit(sentence, txt_scale)
    square = (OWN, OWN)
    diagonal = lax.broadcasted_iota(jnp.int32, square, 0) == lax.broadcasted_iota(jnp.int32, square, 1)
    spread = jnp.broadcast_to(ids[...].astype(jnp.float32), square)
    number = jnp.sum(jnp.where(diagonal, spread, 0.0), axis=1, keepdims=True)
    high = jnp.floor(number * (1 / 128))
    lane = lax.broadcasted_iota(jnp.int32, (OWN, LANES), 1)
    tail = jnp.where(lane == 0, high, jnp.where(lane == 1, number - high * 128, 0.0))
    none = jnp.zeros_like(tail)
    own[:, :width] = jnp.where(holds_images, img, txt).astype(jnp.bfloat16)
    own[:, width:] = jnp.where(holds_images, none, tail).astype(jnp.bfloat16)
    given[:, :width] = jnp.where(holds_images, txt, img).astype(jnp.bfloat16)
    given[:, width:] = jnp.where(holds_images, tail, none).astype(jnp.bfloat16)


def pack_rows(photo_features, sentence_features, ids):
    rows, width = photo_features.shape
    block = jax.ShapeDtypeStruct((rows, width + LANES), jnp.bfloat16)
    scale = jax.ShapeDtypeStruct((rows, 1), jnp.float32)
    return pl.pallas_call(
        pack_kernel,
        out_shape=(block, block, scale, scale),
        in_specs=[pl.BlockSpec(memory_space=pltpu.HBM)] * 3,
        scratch_shapes=[
            pltpu.VMEM((rows, width), photo_features.dtype),
            pltpu.VMEM((rows, width), sentence_features.dtype),
            pltpu.VMEM((1, rows), ids.dtype),
            pltpu.SemaphoreType.DMA((3,)),
        ],
        compiler_params=pltpu.CompilerParams(vmem_limit_bytes=2 << 20),
        name="pack_rows",
    )(
        *(
            pltpu.with_memory_space_constraint(a, pltpu.HBM)
            for a in (photo_features, sentence_features, ids.reshape(1, rows))
        )
    )


def back_through(raw, scale, upstream):
    unit = raw.astype(jnp.float32) * scale
    inner = jnp.sum(unit * upstream, axis=1, keepdims=True)
    return scale * (upstream - unit * inner)


def cat(*parts):
    return jnp.concatenate(parts, axis=0)


def image_ids(z, y):
    row = lax.iota(jnp.int32, 16 * CHIP)
    group, zslot, r = row // (4 * CHIP), row // CHIP % 4, row % CHIP
    owner_z = z ^ jnp.where(zslot % 2 == 1, 8, 0) ^ jnp.where(zslot >= 2, 2, 0)
    owner = device_at(owner_z, group, y, r // OWN)
    return owner * OWN + r % OWN


def text_ids(tail):
    place = lax.broadcasted_iota(jnp.int32, tail.shape, 1)
    weight = jnp.where(place == 0, 128.0, jnp.where(place == 1, 1.0, 0.0))
    return jnp.sum(tail.astype(jnp.float32) * weight, axis=1).astype(jnp.int32)


def shards(
    photo_features, sentence_features, described_photo_number, logit_multiplier, logit_offset
):
    low = lax.axis_index("row")
    rest = lax.axis_index("col")
    z, y = (rest >> 5) * 16 + low, (rest >> 1) & 3
    holds_images = (rest & 1) == 0

    width = photo_features.shape[1]
    block_own, block_given, img_scale, txt_scale = pack_rows(
        photo_features, sentence_features, described_photo_number
    )

    with jax.named_scope("pair_swap"):
        block = cat(block_own, swap_cores(block_given))
    with jax.named_scope("gather_z_far"):
        block = cat(block, z_far(block))
    with jax.named_scope("gather_z_mid"):
        block = cat(block, z_mid(block))
    with jax.named_scope("gather_ring"):
        block = lax.optimization_barrier(block)
        held = around(jnp.tile(block, (8, 1)))
        first, second = held[: 16 * CHIP], held[16 * CHIP :]
    stands_first = (z == 0) | ((z % 2 == 1) & (z < NZ - 1))
    with jax.named_scope("tile_swap"):
        away_first = jnp.where(holds_images, stands_first, True)
        held = jnp.where(holds_images & stands_first, first, second)
        crossed = swap_cores(jnp.where(away_first, first, second))

    mine, other = held[:, :width], crossed[:, :width]
    img_ids = image_ids(z, y)
    mine_ids = jnp.where(holds_images, img_ids, text_ids(held[:, width:]))
    other_ids = jnp.where(holds_images, text_ids(crossed[:, width:]), img_ids)

    logits = (
        logit_multiplier
        * jnp.einsum("od,md->om", other, mine, preferred_element_type=jnp.float32)
        + logit_offset
    )
    sign = jnp.where(other_ids[:, None] == mine_ids[None, :], 1.0, -1.0).astype(jnp.float32)
    weights = (logit_multiplier * -sign * jax.nn.sigmoid(-sign * logits)).astype(jnp.bfloat16)
    away = jnp.dot(weights, mine, preferred_element_type=jnp.float32).astype(jnp.bfloat16)
    home = jnp.einsum("om,od->md", weights, other, preferred_element_type=jnp.float32)

    with jax.named_scope("tile_sum"):
        crossed = swap_cores(away).astype(jnp.float32)
        imgs, none = home + crossed, jnp.zeros_like(home)
        first = jnp.where(holds_images, jnp.where(stands_first, imgs, none), crossed)
        second = jnp.where(holds_images, jnp.where(stands_first, none, imgs), home)
    with jax.named_scope("ring_sum"):
        parts = around(cat(first.astype(jnp.bfloat16), second.astype(jnp.bfloat16)))
        total = jnp.sum(parts.reshape(8, 4 * CHIP, width).astype(jnp.float32), axis=0)
    for name, swap in (("z_mid_sum", z_mid), ("z_far_sum", z_far)):
        with jax.named_scope(name):
            rows = total.shape[0] // 2
            total = total[:rows] + swap(total[rows:].astype(jnp.bfloat16)).astype(jnp.float32)
    with jax.named_scope("pair_return"):
        kept, given = total[:OWN], swap_cores(total[OWN:])
    return (
        back_through(photo_features, img_scale, jnp.where(holds_images, kept, given)),
        back_through(sentence_features, txt_scale, jnp.where(holds_images, given, kept)),
    )


def solution(mesh):
    placed = (P(("row", "col"), None), P(("row", "col"), None), P(("row", "col")), P(), P())
    return jax.shard_map(
        shards,
        mesh=mesh,
        in_specs=placed,
        out_specs=(P(("row", "col"), None), P(("row", "col"), None)),
        check_vma=False,
    )
```

```python
import jax
import jax.numpy as jnp
from jax import lax
from jax.experimental import pallas as pl
from jax.experimental.pallas import tpu as pltpu
from jax.sharding import PartitionSpec as P

NZ, NX, NY = 32, 4, 4
OWN = 12
CHIP = 2 * OWN
LANES = 128
BOTH = ("row", "col")


def device_at(z, x, y, c):
    return (z & 15) * 64 + (z >> 4) * 32 + x * 8 + y * 2 + c


def permute(value, images=None, texts=None):
    pairs = []
    for z in range(NZ):
        for x in range(NX):
            for y in range(NY):
                for c, to in enumerate((images, texts)):
                    if to is not None:
                        pairs.append((device_at(z, x, y, c), device_at(*to(z, x, y), c)))
    return lax.ppermute(value, BOTH, pairs)


def z_far(value):
    return permute(
        value,
        lambda z, x, y: (z ^ 8, x, y),
        lambda z, x, y: ((((z + 8) % NZ) ^ 8) - 8 & (NZ - 1), x, y),
    )


def z_mid(value):
    return permute(value, lambda z, x, y: (z ^ 2, x, y), lambda z, x, y: (z ^ 4, x, y))


def eights():
    groups, seen = [], set()
    for z in range(NZ):
        for k in range(4):
            for c in range(2):
                if (z, k, c) in seen:
                    continue
                pair = (z, z ^ 1) if c else (z, (z + 1 if z % 2 else z - 1) % NZ)
                seen.update((w, k, c) for w in pair)
                groups.append([device_at(w, *((k, n) if c else (n, k)), c) for w in pair for n in range(4)])
    return groups


EIGHTS = eights()


def around(value):
    return lax.all_to_all(value, BOTH, 0, 0, axis_index_groups=EIGHTS, tiled=True)


def swap_cores(value):
    n = NZ * NX * NY * 2
    return lax.ppermute(value, BOTH, [(d, d ^ 1) for d in range(n)])


def pack_kernel(
    photo_in, sentence_in, ids_in, own, given, img_scale, txt_scale, photo, sentence, ids, arrived
):
    copies = [
        pltpu.make_async_copy(source, target, arrived.at[k])
        for k, (source, target) in enumerate(
            ((photo_in, photo), (sentence_in, sentence), (ids_in, ids))
        )
    ]
    for copy in copies:
        copy.start()
    for copy in copies:
        copy.wait()
    width = photo.shape[1]
    holds_images = lax.axis_index("col") % 2 == 0

    def unit(raw, scale):
        values = raw[...].astype(jnp.float32)
        scale[...] = lax.rsqrt(jnp.sum(values * values, axis=1, keepdims=True) + 1e-06)
        return values * scale[...]

    img, txt = unit(photo, img_scale), unit(sentence, txt_scale)
    square = (OWN, OWN)
    diagonal = lax.broadcasted_iota(jnp.int32, square, 0) == lax.broadcasted_iota(jnp.int32, square, 1)
    spread = jnp.broadcast_to(ids[...].astype(jnp.float32), square)
    number = jnp.sum(jnp.where(diagonal, spread, 0.0), axis=1, keepdims=True)
    high = jnp.floor(number * (1 / 128))
    lane = lax.broadcasted_iota(jnp.int32, (OWN, LANES), 1)
    tail = jnp.where(lane == 0, high, jnp.where(lane == 1, number - high * 128, 0.0))
    none = jnp.zeros_like(tail)
    own[:, :width] = jnp.where(holds_images, img, txt).astype(jnp.bfloat16)
    own[:, width:] = jnp.where(holds_images, none, tail).astype(jnp.bfloat16)
    given[:, :width] = jnp.where(holds_images, txt, img).astype(jnp.bfloat16)
    given[:, width:] = jnp.where(holds_images, tail, none).astype(jnp.bfloat16)


def copies_kernel(block, out):
    rows = block.shape[0]
    for k in range(out.shape[0] // rows):
        out[k * rows : (k + 1) * rows, :] = block[...]


def eight_copies(block):
    rows, width = block.shape
    return pl.pallas_call(
        copies_kernel,
        out_shape=jax.ShapeDtypeStruct((8 * rows, width), block.dtype),
        compiler_params=pltpu.CompilerParams(vmem_limit_bytes=4 << 20),
        name="eight_copies",
    )(block)


def pack_rows(photo_features, sentence_features, ids):
    rows, width = photo_features.shape
    block = jax.ShapeDtypeStruct((rows, width + LANES), jnp.bfloat16)
    scale = jax.ShapeDtypeStruct((rows, 1), jnp.float32)
    return pl.pallas_call(
        pack_kernel,
        out_shape=(block, block, scale, scale),
        in_specs=[pl.BlockSpec(memory_space=pltpu.HBM)] * 3,
        scratch_shapes=[
            pltpu.VMEM((rows, width), photo_features.dtype),
            pltpu.VMEM((rows, width), sentence_features.dtype),
            pltpu.VMEM((1, rows), ids.dtype),
            pltpu.SemaphoreType.DMA((3,)),
        ],
        compiler_params=pltpu.CompilerParams(vmem_limit_bytes=2 << 20),
        name="pack_rows",
    )(
        *(
            pltpu.with_memory_space_constraint(a, pltpu.HBM)
            for a in (photo_features, sentence_features, ids.reshape(1, rows))
        )
    )


def back_through(raw, scale, upstream):
    unit = raw.astype(jnp.float32) * scale
    inner = jnp.sum(unit * upstream, axis=1, keepdims=True)
    return scale * (upstream - unit * inner)


def cat(*parts):
    return jnp.concatenate(parts, axis=0)


def image_ids(z, y):
    row = lax.iota(jnp.int32, 16 * CHIP)
    group, zslot, r = row // (4 * CHIP), row // CHIP % 4, row % CHIP
    owner_z = z ^ jnp.where(zslot % 2 == 1, 8, 0) ^ jnp.where(zslot >= 2, 2, 0)
    owner = device_at(owner_z, group, y, r // OWN)
    return owner * OWN + r % OWN


def text_ids(tail):
    place = lax.broadcasted_iota(jnp.int32, tail.shape, 1)
    weight = jnp.where(place == 0, 128.0, jnp.where(place == 1, 1.0, 0.0))
    return jnp.sum(tail.astype(jnp.float32) * weight, axis=1).astype(jnp.int32)


def shards(
    photo_features, sentence_features, described_photo_number, logit_multiplier, logit_offset
):
    low = lax.axis_index("row")
    rest = lax.axis_index("col")
    z, y = (rest >> 5) * 16 + low, (rest >> 1) & 3
    holds_images = (rest & 1) == 0

    width = photo_features.shape[1]
    block_own, block_given, img_scale, txt_scale = pack_rows(
        photo_features, sentence_features, described_photo_number
    )

    with jax.named_scope("pair_swap"):
        block = cat(block_own, swap_cores(block_given))
    with jax.named_scope("gather_z_far"):
        block = cat(block, z_far(block))
    with jax.named_scope("gather_z_mid"):
        block = cat(block, z_mid(block))
    with jax.named_scope("gather_ring"):
        held = around(eight_copies(block))
        first, second = held[: 16 * CHIP], held[16 * CHIP :]
    stands_first = (z == 0) | ((z % 2 == 1) & (z < NZ - 1))
    with jax.named_scope("tile_swap"):
        away_first = jnp.where(holds_images, stands_first, True)
        held = jnp.where(holds_images & stands_first, first, second)
        crossed = swap_cores(jnp.where(away_first, first, second))

    mine, other = held[:, :width], crossed[:, :width]
    img_ids = image_ids(z, y)
    mine_ids = jnp.where(holds_images, img_ids, text_ids(held[:, width:]))
    other_ids = jnp.where(holds_images, text_ids(crossed[:, width:]), img_ids)

    logits = (
        logit_multiplier
        * jnp.einsum("od,md->om", other, mine, preferred_element_type=jnp.float32)
        + logit_offset
    )
    sign = jnp.where(other_ids[:, None] == mine_ids[None, :], 1.0, -1.0).astype(jnp.float32)
    weights = (logit_multiplier * -sign * jax.nn.sigmoid(-sign * logits)).astype(jnp.bfloat16)
    away = jnp.dot(weights, mine, preferred_element_type=jnp.float32).astype(jnp.bfloat16)
    home = jnp.einsum("om,od->md", weights, other, preferred_element_type=jnp.float32)

    with jax.named_scope("tile_sum"):
        crossed = swap_cores(away).astype(jnp.float32)
        imgs, none = home + crossed, jnp.zeros_like(home)
        first = jnp.where(holds_images, jnp.where(stands_first, imgs, none), crossed)
        second = jnp.where(holds_images, jnp.where(stands_first, none, imgs), home)
    with jax.named_scope("ring_sum"):
        parts = around(cat(first.astype(jnp.bfloat16), second.astype(jnp.bfloat16)))
        total = jnp.sum(parts.reshape(8, 4 * CHIP, width).astype(jnp.float32), axis=0)
    for name, swap in (("z_mid_sum", z_mid), ("z_far_sum", z_far)):
        with jax.named_scope(name):
            rows = total.shape[0] // 2
            total = total[:rows] + swap(total[rows:].astype(jnp.bfloat16)).astype(jnp.float32)
    with jax.named_scope("pair_return"):
        kept, given = total[:OWN], swap_cores(total[OWN:])
    return (
        back_through(photo_features, img_scale, jnp.where(holds_images, kept, given)),
        back_through(sentence_features, txt_scale, jnp.where(holds_images, given, kept)),
    )


def solution(mesh):
    placed = (P(("row", "col"), None), P(("row", "col"), None), P(("row", "col")), P(), P())
    return jax.shard_map(
        shards,
        mesh=mesh,
        in_specs=placed,
        out_specs=(P(("row", "col"), None), P(("row", "col"), None)),
        check_vma=False,
    )
```

```python
import jax
import jax.numpy as jnp
from jax import lax
from jax.experimental import pallas as pl
from jax.experimental.pallas import tpu as pltpu
from jax.sharding import PartitionSpec as P

NZ, NX, NY = 32, 4, 4
OWN = 12
CHIP = 2 * OWN
LANES = 128
BOTH = ("row", "col")


def device_at(z, x, y, c):
    return (z & 15) * 64 + (z >> 4) * 32 + x * 8 + y * 2 + c


def permute(value, images=None, texts=None):
    pairs = []
    for z in range(NZ):
        for x in range(NX):
            for y in range(NY):
                for c, to in enumerate((images, texts)):
                    if to is not None:
                        pairs.append((device_at(z, x, y, c), device_at(*to(z, x, y), c)))
    return lax.ppermute(value, BOTH, pairs)


def z_far(value):
    return permute(
        value,
        lambda z, x, y: (z ^ 8, x, y),
        lambda z, x, y: ((((z + 8) % NZ) ^ 8) - 8 & (NZ - 1), x, y),
    )


def z_mid(value):
    return permute(value, lambda z, x, y: (z ^ 2, x, y), lambda z, x, y: (z ^ 4, x, y))


def eights():
    groups, seen = [], set()
    for z in range(NZ):
        for k in range(4):
            for c in range(2):
                if (z, k, c) in seen:
                    continue
                pair = (z, z ^ 1) if c else (z, (z + 1 if z % 2 else z - 1) % NZ)
                seen.update((w, k, c) for w in pair)
                groups.append([device_at(w, *((k, n) if c else (n, k)), c) for w in pair for n in range(4)])
    return groups


EIGHTS = eights()


def around(value):
    return lax.all_to_all(value, BOTH, 0, 0, axis_index_groups=EIGHTS, tiled=True)


def swap_cores(value):
    n = NZ * NX * NY * 2
    return lax.ppermute(value, BOTH, [(d, d ^ 1) for d in range(n)])


def pack_kernel(
    photo_in, sentence_in, ids_in, own, given, img_scale, txt_scale, photo, sentence, ids, arrived
):
    copies = [
        pltpu.make_async_copy(source, target, arrived.at[k])
        for k, (source, target) in enumerate(
            ((photo_in, photo), (sentence_in, sentence), (ids_in, ids))
        )
    ]
    for copy in copies:
        copy.start()
    for copy in copies:
        copy.wait()
    width = photo.shape[1]
    holds_images = lax.axis_index("col") % 2 == 0

    def unit(raw, scale):
        values = raw[...].astype(jnp.float32)
        scale[...] = lax.rsqrt(jnp.sum(values * values, axis=1, keepdims=True) + 1e-06)
        return values * scale[...]

    img, txt = unit(photo, img_scale), unit(sentence, txt_scale)
    square = (OWN, OWN)
    diagonal = lax.broadcasted_iota(jnp.int32, square, 0) == lax.broadcasted_iota(jnp.int32, square, 1)
    spread = jnp.broadcast_to(ids[...].astype(jnp.float32), square)
    number = jnp.sum(jnp.where(diagonal, spread, 0.0), axis=1, keepdims=True)
    high = jnp.floor(number * (1 / 128))
    lane = lax.broadcasted_iota(jnp.int32, (OWN, LANES), 1)
    tail = jnp.where(lane == 0, high, jnp.where(lane == 1, number - high * 128, 0.0))
    none = jnp.zeros_like(tail)
    own[:, :width] = jnp.where(holds_images, img, txt).astype(jnp.bfloat16)
    own[:, width:] = jnp.where(holds_images, none, tail).astype(jnp.bfloat16)
    given[:, :width] = jnp.where(holds_images, txt, img).astype(jnp.bfloat16)
    given[:, width:] = jnp.where(holds_images, tail, none).astype(jnp.bfloat16)


def copies_kernel(block, out):
    rows = block.shape[0]
    for k in range(out.shape[0] // rows):
        out[k * rows : (k + 1) * rows, :] = block[...]


def eight_copies(block):
    rows, width = block.shape
    return pl.pallas_call(
        copies_kernel,
        out_shape=jax.ShapeDtypeStruct((8 * rows, width), block.dtype),
        compiler_params=pltpu.CompilerParams(vmem_limit_bytes=4 << 20),
        name="eight_copies",
    )(block)


def pack_rows(photo_features, sentence_features, ids):
    rows, width = photo_features.shape
    block = jax.ShapeDtypeStruct((rows, width + LANES), jnp.bfloat16)
    scale = jax.ShapeDtypeStruct((rows, 1), jnp.float32)
    return pl.pallas_call(
        pack_kernel,
        out_shape=(block, block, scale, scale),
        in_specs=[pl.BlockSpec(memory_space=pltpu.HBM)] * 3,
        scratch_shapes=[
            pltpu.VMEM((rows, width), photo_features.dtype),
            pltpu.VMEM((rows, width), sentence_features.dtype),
            pltpu.VMEM((1, rows), ids.dtype),
            pltpu.SemaphoreType.DMA((3,)),
        ],
        compiler_params=pltpu.CompilerParams(vmem_limit_bytes=2 << 20),
        name="pack_rows",
    )(
        *(
            pltpu.with_memory_space_constraint(a, pltpu.HBM)
            for a in (photo_features, sentence_features, ids.reshape(1, rows))
        )
    )


def back_through(raw, scale, upstream):
    unit = raw.astype(jnp.float32) * scale
    inner = jnp.sum(unit * upstream, axis=1, keepdims=True)
    return scale * (upstream - unit * inner)


def cat(*parts):
    return jnp.concatenate(parts, axis=0)


def image_ids(z, y):
    row = lax.iota(jnp.int32, 16 * CHIP)
    group, zslot, r = row // (4 * CHIP), row // CHIP % 4, row % CHIP
    owner_z = z ^ jnp.where(zslot % 2 == 1, 8, 0) ^ jnp.where(zslot >= 2, 2, 0)
    owner = device_at(owner_z, group, y, r // OWN)
    return owner * OWN + r % OWN


def text_ids(tail):
    place = lax.broadcasted_iota(jnp.int32, tail.shape, 1)
    weight = jnp.where(place == 0, 128.0, jnp.where(place == 1, 1.0, 0.0))
    return jnp.sum(tail.astype(jnp.float32) * weight, axis=1).astype(jnp.int32)


def shards(
    photo_features, sentence_features, described_photo_number, logit_multiplier, logit_offset
):
    low = lax.axis_index("row")
    rest = lax.axis_index("col")
    z, y = (rest >> 5) * 16 + low, (rest >> 1) & 3
    holds_images = (rest & 1) == 0

    width = photo_features.shape[1]
    block_own, block_given, img_scale, txt_scale = pack_rows(
        photo_features, sentence_features, described_photo_number
    )

    with jax.named_scope("pair_swap"):
        block = cat(block_own, swap_cores(block_given))
    with jax.named_scope("gather_z_far"):
        block = cat(block, z_far(block))
    with jax.named_scope("gather_z_mid"):
        block = cat(block, z_mid(block))
    with jax.named_scope("gather_ring"):
        held = around(eight_copies(block))
        first, second = held[: 16 * CHIP], held[16 * CHIP :]
    stands_first = (z == 0) | ((z % 2 == 1) & (z < NZ - 1))
    with jax.named_scope("tile_swap"):
        away_first = jnp.where(holds_images, stands_first, True)
        held = jnp.where(holds_images & stands_first, first, second)
        crossed = swap_cores(jnp.where(away_first, first, second))

    mine, other = held[:, :width], crossed[:, :width]
    img_ids = image_ids(z, y)
    mine_ids = jnp.where(holds_images, img_ids, text_ids(held[:, width:]))
    other_ids = jnp.where(holds_images, text_ids(crossed[:, width:]), img_ids)

    logits = (
        logit_multiplier
        * jnp.einsum("od,md->om", other, mine, preferred_element_type=jnp.float32)
        + logit_offset
    )
    sign = jnp.where(other_ids[:, None] == mine_ids[None, :], 1.0, -1.0).astype(jnp.float32)
    weights = (logit_multiplier * -sign * jax.nn.sigmoid(-sign * logits)).astype(jnp.bfloat16)
    away = jnp.dot(weights, mine, preferred_element_type=jnp.float32).astype(jnp.bfloat16)
    home = jnp.einsum("om,od->md", weights, other, preferred_element_type=jnp.float32)

    with jax.named_scope("tile_sum"):
        crossed = swap_cores(away).astype(jnp.float32)
        home = lax.optimization_barrier(home)
        imgs, none = home + crossed, jnp.zeros_like(home)
        first = jnp.where(holds_images, jnp.where(stands_first, imgs, none), crossed)
        second = jnp.where(holds_images, jnp.where(stands_first, none, imgs), home)
    with jax.named_scope("ring_sum"):
        parts = around(cat(first.astype(jnp.bfloat16), second.astype(jnp.bfloat16)))
        total = jnp.sum(parts.reshape(8, 4 * CHIP, width).astype(jnp.float32), axis=0)
    for name, swap in (("z_mid_sum", z_mid), ("z_far_sum", z_far)):
        with jax.named_scope(name):
            rows = total.shape[0] // 2
            total = total[:rows] + swap(total[rows:].astype(jnp.bfloat16)).astype(jnp.float32)
    with jax.named_scope("pair_return"):
        kept, given = total[:OWN], swap_cores(total[OWN:])
    return (
        back_through(photo_features, img_scale, jnp.where(holds_images, kept, given)),
        back_through(sentence_features, txt_scale, jnp.where(holds_images, given, kept)),
    )


def solution(mesh):
    placed = (P(("row", "col"), None), P(("row", "col"), None), P(("row", "col")), P(), P())
    return jax.shard_map(
        shards,
        mesh=mesh,
        in_specs=placed,
        out_specs=(P(("row", "col"), None), P(("row", "col"), None)),
        check_vma=False,
    )
```
